256 devices in a mesh: blk: 64 (over z, x, y_lo), jac: 4 (over y_hi, core).
Axes of the slice: x: 4, y: 4 (y_hi: 2, y_lo: 2; y = y_hi * 2 + y_lo), z: 8, core: 2. Of those that a mesh axis runs over, the one named last changes fastest.
Arguments:
- coefficients: bfloat16 [16384, 4096], P('blk', 'jac'), may hold values from -0.09375 to 0.09375
- jacobi_matrix: bfloat16 [4096, 4096], P(None, 'jac'), may hold values from -12 to 12, as said below
- jac_limit: int32 [16384], P('blk'), may hold values from 1024 to 4096, as said below
Outputs:
- band_out: float32 [16384, 33, 256], P(('blk', 'jac'))
The draws below stay inside these ranges and needn't reach their ends.
Inputs may be any that keep to these rules, and one draw needn't show every extreme that they name: `jac_limit`: every value from 1024 to 4096 may occur; both ends occur in every draw. `jacobi_matrix`: Symmetric.
All inputs are finite; a program needn't handle non-finite values.
Results may differ from the reference program's by a relative error of at most 0.0029.
Values may be sent and summed in bfloat16 or wider, within the bound.
No kernel may reach another device: no remote copies, remote signals or barrier semaphores. Data moves between devices by JAX's collectives and lax.ppermute only.
A program may use at most 64 MiB of HBM per device.

```python
import jax
import jax.numpy as jnp
from jax import lax

JACOBI = 4096
TRIP_DEV = 256
BLOCKS = 64
HALF_CYCLE = 32
BAND = 33
TRIPLES = 16384


def draw_jacobi_matrix(key, part):
    key = jax.random.fold_in(key, 7)
    key_entries = jax.random.fold_in(key, 0)
    entries = jax.random.normal(key_entries, (JACOBI, JACOBI), jnp.float32)
    return jnp.clip((entries + entries.T) * 0.70710678, -12.0, 12.0).astype(jnp.bfloat16)


def draw_jac_limit(key, part):
    key = jax.random.fold_in(key, 11)
    key_values, key_place = jax.random.split(key)
    limits = jax.random.randint(key_values, (TRIPLES,), JACOBI // 4, JACOBI + 1)
    location = jax.random.randint(key_place, (), 0, TRIPLES)
    limits = limits.at[location].set(JACOBI)
    limits = limits.at[(location + TRIPLES // 2) % TRIPLES].set(JACOBI // 4)
    return limits.astype(jnp.int32)


def level_of(rng, shape, pieces, smallest, top_value):
    factor_of = 1.0
    for position, parts in pieces:
        steps = jax.random.uniform(jax.random.fold_in(jax.random.fold_in(rng, 6), position), (parts,), jnp.float32, smallest / len(pieces), top_value / len(pieces))
        factor_of = factor_of * jnp.repeat(jnp.exp(steps), shape[position] // parts).reshape((-1,) + (1,) * (len(shape) - 1 - position))
    return factor_of


def bell_draw(key, dims, width, bound, cuts=(), kind=jnp.bfloat16):
    values = width * jax.random.normal(key, dims, jnp.float32)
    if cuts:
        values = values * level_of(key, dims, cuts, -0.22, 0.18)
    return jnp.clip(values, -bound, bound).astype(kind)


def setup_inputs(seed: int = 0) -> dict:
    keys = jax.random.split(jax.random.key(seed), 4)
    return {
        "coefficients": bell_draw(keys[0], (TRIPLES, JACOBI), JACOBI ** -0.5, 0.09375, ((0, 64), (1, 4))),
        "jacobi_matrix": draw_jacobi_matrix(jax.random.fold_in(keys[3], 71), 0),
        "jac_limit": draw_jac_limit(jax.random.fold_in(keys[3], 71), 0),
    }


def reference(coefficients, jacobi_matrix, jac_limit):
    columns = lax.broadcasted_iota(jnp.int32, (TRIPLES, JACOBI), 1)
    masked = jnp.where(columns < jac_limit[:, None], coefficients, jnp.zeros_like(coefficients))
    product = jnp.dot(masked, jacobi_matrix, preferred_element_type=jnp.float32).astype(jnp.bfloat16)
    stacked = masked.reshape(BLOCKS, TRIP_DEV, JACOBI)
    shifts = jnp.arange(BAND, dtype=jnp.int32)

    def one_block(block_index):
        own_rows = lax.dynamic_slice_in_dim(product, (block_index * TRIP_DEV).astype(jnp.int32), TRIP_DEV, 0)
        partners = ((block_index + shifts) % BLOCKS).astype(jnp.int32)
        chosen = jnp.take(stacked, partners, axis=0).reshape(BAND * TRIP_DEV, JACOBI)
        tiles = lax.dot_general(own_rows, chosen, (((1,), (1,)), ((), ())), preferred_element_type=jnp.float32)
        tiles = tiles.reshape(TRIP_DEV, BAND, TRIP_DEV)
        keep_tile = jnp.logical_or(shifts < HALF_CYCLE, block_index < HALF_CYCLE)
        return jnp.where(keep_tile[None, :, None], tiles, jnp.zeros_like(tiles))

    result = lax.map(one_block, jnp.arange(BLOCKS, dtype=jnp.int32))
    return result.reshape(TRIPLES, BAND, TRIP_DEV)
```

```python
import functools

import jax
import jax.numpy as jnp
from jax import lax
from jax.experimental import pallas as pl
from jax.experimental.pallas import tpu as pltpu
from jax.sharding import Mesh, PartitionSpec as P

DEPTH = 5
WIDE = 4


def shift(block, axis, distance):
    n = lax.axis_size(axis)
    return lax.ppermute(block, axis, [((i + distance) % n, i) for i in range(n)])


def tiles(late, products, panels, start, rows, extra, adds, dtype):
    count, tile = len(products), panels[0].shape[0]
    columns = (count * WIDE + extra) * tile

    def kernel(late_ref, *refs):
        product_refs, panel_refs = refs[:count], refs[count : count + DEPTH]
        add_refs, out_ref = refs[count + DEPTH : -1], refs[-1]

        def put(row, column, panel):
            result = lax.dot_general(
                product_refs[row][start : start + rows, :],
                panel_refs[panel][...],
                (((1,), (1,)), ((), ())),
                preferred_element_type=jnp.float32,
            )
            at = slice(column * tile, (column + 1) * tile)
            for ref, (_, first) in zip(add_refs, adds):
                result += ref[first : first + rows, at].astype(jnp.float32)
            out_ref[:, at] = result.astype(out_ref.dtype)

        for row in range(count):
            for skip in (0, 1):

                @pl.when(late_ref[row] == skip)
                def _(row=row, skip=skip):
                    for step in range(WIDE):
                        put(row, row * WIDE + step, step + skip)

        if extra:
            put(0, count * WIDE, DEPTH - 1)

    depth = panels[0].shape[1]
    flops = 2 * rows * columns * depth
    moved = 2 * depth * (count * rows + DEPTH * tile) + 4 * rows * columns
    return pl.pallas_call(
        kernel,
        out_shape=jax.ShapeDtypeStruct((rows, columns), dtype),
        in_specs=[pl.BlockSpec(memory_space=pltpu.SMEM)]
        + [pl.BlockSpec(memory_space=pltpu.VMEM)] * (count + DEPTH + len(adds)),
        out_specs=pl.BlockSpec(memory_space=pltpu.VMEM),
        compiler_params=pltpu.CompilerParams(vmem_limit_bytes=32 * 2**20),
        cost_estimate=pl.CostEstimate(flops=flops, bytes_accessed=moved, transcendentals=0),
    )(late, *products, *panels, *[array for array, _ in adds])


def per_device(coefficients, jacobi_matrix, jac_limit):
    tile, width = coefficients.shape
    z, x, l = (lax.axis_index(name) for name in "zxl")
    h, c = lax.axis_index("h"), lax.axis_index("c")
    quarter = 2 * h + c
    columns = quarter * width + lax.broadcasted_iota(jnp.int32, (tile, width), 1)
    masked = jnp.where(columns < jac_limit[:, None], coefficients, jnp.zeros_like(coefficients))

    def part(panel, other):
        rows = lax.dynamic_slice_in_dim(jacobi_matrix, (quarter ^ other) * width, width, 0)
        return jnp.dot(panel, rows, preferred_element_type=jnp.float32)

    across = shift(masked, "h", 1)
    beside = shift(masked, "c", 1)
    total = part(masked, 0) + part(beside, 1)
    total = total + part(across, 2) + part(shift(across, "c", 1), 3)
    product = total.astype(jnp.bfloat16)
    share = tile // 4
    product = jnp.concatenate(
        [
            lax.dynamic_slice_in_dim(product, (quarter ^ other) * share, share, 0)
            for other in (1, 3, 2, 0)
        ]
    )

    panels = [masked]
    for _ in range(DEPTH - 1):
        panels.append(shift(panels[-1], "z", 1))

    flip = shift(product, "l", 1)
    up, down = shift(product, "x", 1), shift(product, "x", -1)
    up_flip, down_flip = shift(up, "l", 1), shift(flip, "x", -1)
    far = shift(up, "x", 1)
    half = tile // 2
    far_flip = jnp.concatenate(
        [shift(up_flip[:half], "x", 1), shift(down_flip[half:], "x", -1)]
    )

    def late(dx, dl):
        place = 2 * ((x + dx) % 4) + (l ^ dl)
        return (place > 2 * x + l).astype(jnp.int32)

    def to(block, dx, dl):
        pairs = [
            (2 * i + j, 2 * ((i + dx) % 4) + (j ^ dl)) for i in range(4) for j in range(2)
        ]
        return lax.ppermute(block, ("x", "l"), pairs)

    got = {}
    groups = (
        (((0, 0), (0, 1), (1, 0), (-1, 0)), (product, flip, up, down)),
        (((1, 1), (-1, 1), (2, 0), (2, 1)), (up_flip, down_flip, far, far_flip)),
    )
    for places, products in groups:
        extra = int(places[0] == (0, 0))
        lates = jnp.stack([late(*place) for place in places])
        run = functools.partial(tiles, lates, products, panels, extra=extra)
        sent = run(start=0, rows=2 * share, adds=(), dtype=jnp.bfloat16)
        core = shift(sent, "c", 1)
        sent = run(start=2 * share, rows=share, adds=((core, share),), dtype=jnp.bfloat16)
        other = shift(sent, "h", 1)
        kept = run(start=3 * share, rows=share, adds=((core, 0),), dtype=jnp.float32)
        total = kept + other.astype(jnp.float32)
        for index, (dx, dl) in enumerate(places):
            piece = total[:, index * WIDE * tile : (index + 1) * WIDE * tile]
            if (dx, dl) != (0, 0):
                piece = to(piece.astype(jnp.bfloat16), dx, dl)
            got[-dx % 4, dl] = piece
        if extra:
            last = total[:, len(places) * WIDE * tile :]

    last = jnp.where(z < lax.axis_size("z") // 2, last, jnp.zeros_like(last))

    def piece_at(m):
        if m % 2 == 0:
            return got[m // 2, 0]
        return jnp.where(l == 0, got[m // 2, 1], got[(m + 1) // 2 % 4, 1])

    pieces = [piece_at(m).astype(jnp.float32) for m in range(8)]
    out = [pieces[m][:, e * tile : (e + 1) * tile] for e in range(WIDE) for m in range(8)]
    return jnp.stack([*out, last], axis=1)


def solution(mesh):
    fine = Mesh(mesh.devices.reshape(8, 4, 2, 2, 2), ("z", "x", "l", "h", "c"))
    blk, jac = ("z", "x", "l"), ("h", "c")
    in_specs = (P(blk, jac), P(None, jac), P(blk))
    out_specs = P(blk + jac, None, None)
    return jax.shard_map(
        per_device, mesh=fine, in_specs=in_specs, out_specs=out_specs, check_vma=False
    )
```

```python
import jax
import jax.numpy as jnp
from jax import lax
from jax.experimental import pallas as pl
from jax.experimental.pallas import tpu as pltpu
from jax.sharding import Mesh, PartitionSpec as P

WIDE = 4
VMEM = pl.BlockSpec(memory_space=pltpu.VMEM)
SMEM = pl.BlockSpec(memory_space=pltpu.SMEM)
BF16, F32 = jnp.bfloat16, jnp.float32
TRANSPOSED = (((1,), (1,)), ((), ()))


def shift(block, axis, distance):
    n = lax.axis_size(axis)
    return lax.ppermute(block, axis, [((i + distance) % n, i) for i in range(n)])


def across_and_flip(block):
    return lax.ppermute(block, ("l", "h"), [(i, 3 - i) for i in range(4)])


def call(kernel, out_shape, args, scratch=(), flops=0, limit=20):
    moved = sum(a.size * a.dtype.itemsize for a in args)
    return pl.pallas_call(
        kernel,
        out_shape=out_shape,
        in_specs=[SMEM] + [VMEM] * (len(args) - 1),
        out_specs=jax.tree.map(lambda _: VMEM, out_shape),
        scratch_shapes=list(scratch),
        compiler_params=pltpu.CompilerParams(vmem_limit_bytes=limit * 2**20),
        cost_estimate=pl.CostEstimate(flops=flops, bytes_accessed=moved, transcendentals=0),
    )(*args)


def like(rows, columns, dtype):
    return jax.ShapeDtypeStruct((rows, columns), dtype)


def own_product(place, total, across, across_beside, slab):
    rows, width = total.shape
    share = rows // 4

    def kernel(place_ref, total_ref, a_ref, b_ref, slab_ref, send_ref, keep_ref, sum_ref):
        core, quarter = place_ref[0], place_ref[1]
        mine = slab_ref[pl.ds(pl.multiple_of(core * width, width), width), :]
        theirs = slab_ref[pl.ds(pl.multiple_of((1 - core) * width, width), width), :]
        sum_ref[...] = (
            total_ref[...]
            + jnp.dot(a_ref[...], mine, preferred_element_type=F32)
            + jnp.dot(b_ref[...], theirs, preferred_element_type=F32)
        )
        for ref, others in ((send_ref, (3, 1)), (keep_ref, (2, 0))):
            for to, other in enumerate(others):
                start = pl.multiple_of((quarter ^ other) * share, share)
                ref[to * share : (to + 1) * share, :] = sum_ref[pl.ds(start, share), :].astype(BF16)

    return call(
        kernel,
        [like(rows // 2, width, BF16)] * 2,
        (place, total, across, across_beside, slab),
        scratch=(pltpu.VMEM((rows, width), F32),),
        flops=4 * rows * width * width,
    )


def tiles(late, products, panels, blocks, same, flipped, weight):
    tile, depth = products[0][1].shape
    half, share, n = tile // 2, tile // 4, len(products)
    first = min(steps[0] for _, steps in blocks)
    used = [p for p in range(first, len(panels))]
    flat = [a for _, a in products] + [a for p in used for a in panels[p]]
    most = max(len(members) for members, _ in blocks)
    widest = max(len(steps) for _, steps in blocks) + 1
    n_out = 2 * bool(same) + 2 * bool(flipped)

    def kernel(late_ref, *refs):
        product_refs = {key: refs[i] for i, (key, _) in enumerate(products)}
        panel_refs = {p: refs[n + 2 * i : n + 2 * i + 2] for i, p in enumerate(used)}
        out_refs, (stack_ref, held_ref) = refs[len(flat) : len(flat) + n_out], refs[-2:]
        for members, steps in blocks:
            rows = len(members) * half
            for i, key in enumerate(members):
                for part in range(2):
                    stack_ref[part, i * half : (i + 1) * half, :] = product_refs[key][
                        part * half : (part + 1) * half, :
                    ]
            for i, step in enumerate((*steps, steps[-1] + 1)):
                held_ref[:rows, i * tile : (i + 1) * tile] = sum(
                    lax.dot_general(
                        stack_ref[part, :rows, :],
                        panel_refs[step][part][...],
                        TRANSPOSED,
                        preferred_element_type=F32,
                    )
                    for part in range(2)
                )
            for into, (names, kinds) in enumerate(((same, (BF16, F32)), (flipped, (BF16, BF16)))):
                for slot, (key, step) in enumerate(names):
                    if key not in members or not (step in steps or step == WIDE):
                        continue
                    i = members.index(key)
                    column = step - steps[0]
                    if step < WIDE:
                        column = column + late_ref[key]
                    at = pl.ds(pl.multiple_of(column * tile, tile), tile)
                    theirs = held_ref[i * half : i * half + share, at]
                    ours = held_ref[i * half + share : (i + 1) * half, at]
                    pair = (ours, theirs) if into else (theirs, ours)
                    for ref, value, kind in zip(out_refs[2 * into * bool(same) :], pair, kinds):
                        ref[:, slot * tile : (slot + 1) * tile] = value.astype(kind)

    out = []
    if same:
        out += [like(share, len(same) * tile, BF16), like(share, len(same) * tile, F32)]
    if flipped:
        out += [like(share, len(flipped) * tile, BF16)] * 2
    flops = weight * 2 * half * 2 * depth * tile * (len(same) + len(flipped))
    return call(
        kernel,
        out,
        (late, *flat),
        scratch=(
            pltpu.VMEM((2, most * half, depth), BF16),
            pltpu.VMEM((most * half, widest * tile), F32),
        ),
        flops=flops,
    )


def split(same, flipped, groups, tile):
    share = same[0].shape[0]

    def kernel(_, *refs):
        pairs, out_refs = (refs[:2], refs[2:4]), refs[4:]
        for ref, group in zip(out_refs, groups):
            for to, (which, slot) in enumerate(group):
                left, right = pairs[which]
                at = slice(slot * tile, (slot + 1) * tile)
                value = left[:, at].astype(F32) + right[:, at].astype(F32)
                ref[:, to * tile : (to + 1) * tile] = value.astype(ref.dtype)

    return call(
        kernel,
        [
            like(share, len(group) * tile, BF16 if index else F32)
            for index, group in enumerate(groups)
        ],
        (jnp.zeros((1,), jnp.int32), *same, *flipped),
    )


def assemble(place, arrays, plan, band, share, tile):
    def kernel(place_ref, *refs):
        *refs, out_ref = refs
        low, keep_last = place_ref[0], place_ref[1]
        for ref, entries in zip(refs, plan):
            for slot, entry in enumerate(entries):
                value = ref[:, slot * tile : (slot + 1) * tile].astype(F32)
                if entry is None:
                    out_ref[band - 1] = jnp.where(keep_last > 0, value, jnp.zeros_like(value))
                    continue
                flipped, distance, step = entry
                offset = 2 * distance
                if flipped:
                    offset = (offset + 1 - 2 * low) & 7
                out_ref[offset + 8 * step] = value

    return call(kernel, jax.ShapeDtypeStruct((band, share, tile), F32), (place, *arrays))


def per_device(coefficients, jacobi_matrix, jac_limit):
    tile, width = coefficients.shape
    share = tile // 4
    z, x, l, h, c = (lax.axis_index(name) for name in "zxlhc")
    quarter = 2 * h + c
    hold = lax.optimization_barrier

    columns = quarter * width + lax.broadcasted_iota(jnp.int32, (tile, width), 1)
    masked = jnp.where(columns < jac_limit[:, None], coefficients, jnp.zeros_like(coefficients))

    across = shift(masked, "h", 1)
    panels = [masked, shift(masked, "z", 1)]
    beside = shift(masked, "c", 1)

    def rows_of(index):
        return lax.dynamic_slice_in_dim(jacobi_matrix, index * width, width, 0)

    total = jnp.dot(masked, rows_of(quarter), preferred_element_type=F32)
    total = total + jnp.dot(beside, rows_of(quarter ^ 1), preferred_element_type=F32)
    slab = lax.dynamic_slice_in_dim(jacobi_matrix, (1 - h) * 2 * width, 2 * width, 0)
    total, across, slab, panels[1] = hold((total, across, slab, panels[1]))
    across_beside = shift(across, "c", 1)
    place = jnp.stack([c, quarter]).astype(jnp.int32)
    send, keep = own_product(place, total, across, across_beside, slab)
    product = jnp.concatenate([keep, shift(send, "c", 1)])

    def late(dx, flipped):
        return (2 * ((x + dx) % 4) + (l ^ flipped) > 2 * x + l).astype(jnp.int32)

    distances = (0, 1, -1, 2)
    lates = jnp.stack([late(dx, f) for f in (0, 1) for dx in distances])

    def start(products, panels, blocks, same, flipped, weight):
        flipped = [(4 + d, e) for d, e in flipped]
        return tiles(lates, list(products.items()), panels, blocks, same, flipped, weight)

    def finish(same, flipped, names):
        groups = [
            [(f, s) for f in (0, 1) for s, (d, _) in enumerate(names[f]) if d == to]
            for to in range(4)
        ]
        pieces = split(same, flipped, groups, tile)
        arrays, plan = [], []
        for to, (piece, group) in enumerate(zip(pieces, groups)):
            if to:
                piece = shift(piece, "x", -distances[to])
            arrays.append(piece)
            entries = [(f, names[f][s][1]) for f, s in group]
            plan.append([None if e == WIDE else (f, -distances[to] % 4, e) for f, e in entries])
        return arrays, plan

    panels.append(shift(panels[-1], "z", 1))
    flip = shift(product, "l", 1)
    up, down = shift(product, "x", 1), shift(product, "x", -1)

    flip, up, down, panels[2] = hold((flip, up, down, panels[2]))
    panels.append(shift(panels[-1], "z", 1))
    up_flip, down_flip = shift(up, "l", 1), shift(flip, "x", -1)
    far = shift(up, "x", 1)
    both = [(masked, beside)] + [(p, shift(p, "c", 1)) for p in panels[1:3]]

    up_flip, down_flip, far, panels[3] = hold((up_flip, down_flip, far, panels[3]))
    far_flip = shift(down_flip, "x", -1)
    fourth = shift(panels[3], "z", 1)
    both.append((panels[3], shift(panels[3], "c", 1)))
    same_1 = [(d, e) for d in range(4) for e in range(3)]
    products = {0: product, 1: up, 2: down, 3: far}
    other, own = start(products, both, [((0, 1, 2, 3), (0, 1, 2))], same_1, [], 8)

    flipped_1 = [(d, e) for d in range(3) for e in range(3)]
    flip, _ = hold((flip, other))
    other = shift(other, "h", 1)
    products = {4: flip, 5: up_flip, 6: down_flip}
    by_l, by_both = start(products, both, [((4, 5, 6), (0, 1, 2))], [], flipped_1, 8)
    by_l, by_both = shift(by_l, "l", 1), across_and_flip(by_both)

    both.append(hold((fourth, shift(fourth, "c", 1), other))[:2])
    same_2 = [(0, 3), (1, 3), (2, 3), (3, 3), (0, 4)]
    flipped_2 = [(0, 3), (1, 3), (2, 3), (3, 3), (3, 0), (3, 1), (3, 2)]
    products = {0: product, 1: up, 2: down, 3: far, **products, 7: far_flip}
    blocks = [(tuple(range(8)), (3,)), ((7,), (0, 1, 2))]
    other_2, own_2, by_l_2, by_both_2 = start(products, both, blocks, same_2, flipped_2, 8)
    by_l, by_both, other_2, by_l_2, by_both_2 = hold((by_l, by_both, other_2, by_l_2, by_both_2))
    other_2 = shift(other_2, "h", 1)
    by_l_2, by_both_2 = shift(by_l_2, "l", 1), across_and_flip(by_both_2)
    arrays, plan = finish((own, other), (by_l, by_both), (same_1, flipped_1))
    more, more_plan = finish((own_2, other_2), (by_l_2, by_both_2), (same_2, flipped_2))

    where = jnp.stack([l, (z < lax.axis_size("z") // 2)]).astype(jnp.int32)
    band = 8 * WIDE + 1
    out = assemble(where, arrays + more, plan + more_plan, band, share, tile)
    return jnp.transpose(out, (1, 0, 2))


def solution(mesh):
    fine = Mesh(mesh.devices.reshape(8, 4, 2, 2, 2), ("z", "x", "l", "h", "c"))
    blk, jac = ("z", "x", "l"), ("h", "c")
    in_specs = (P(blk, jac), P(None, jac), P(blk))
    out_specs = P(blk + jac, None, None)
    return jax.shard_map(
        per_device, mesh=fine, in_specs=in_specs, out_specs=out_specs, check_vma=False
    )
```

```python
import jax
import jax.numpy as jnp
from jax import lax
from jax.experimental import pallas as pl
from jax.experimental.pallas import tpu as pltpu
from jax.sharding import Mesh, PartitionSpec as P

WIDE = 4
VMEM = pl.BlockSpec(memory_space=pltpu.VMEM)
SMEM = pl.BlockSpec(memory_space=pltpu.SMEM)
BF16, F32 = jnp.bfloat16, jnp.float32
TRANSPOSED = (((1,), (1,)), ((), ()))


def shift(block, axis, distance):
    n = lax.axis_size(axis)
    return lax.ppermute(block, axis, [((i + distance) % n, i) for i in range(n)])


def across_and_flip(block):
    return lax.ppermute(block, ("l", "h"), [(i, 3 - i) for i in range(4)])


def call(kernel, out_shape, args, scratch=(), flops=0, limit=20):
    moved = sum(a.size * a.dtype.itemsize for a in args)
    return pl.pallas_call(
        kernel,
        out_shape=out_shape,
        in_specs=[SMEM] + [VMEM] * (len(args) - 1),
        out_specs=jax.tree.map(lambda _: VMEM, out_shape),
        scratch_shapes=list(scratch),
        compiler_params=pltpu.CompilerParams(vmem_limit_bytes=limit * 2**20),
        cost_estimate=pl.CostEstimate(flops=flops, bytes_accessed=moved, transcendentals=0),
    )(*args)


def like(rows, columns, dtype):
    return jax.ShapeDtypeStruct((rows, columns), dtype)


def own_product(place, total, across, across_beside, slab):
    rows, width = total.shape
    share = rows // 4

    def kernel(place_ref, total_ref, a_ref, b_ref, slab_ref, send_ref, keep_ref, sum_ref):
        core, quarter = place_ref[0], place_ref[1]
        mine = slab_ref[pl.ds(pl.multiple_of(core * width, width), width), :]
        theirs = slab_ref[pl.ds(pl.multiple_of((1 - core) * width, width), width), :]
        sum_ref[...] = (
            total_ref[...]
            + jnp.dot(a_ref[...], mine, preferred_element_type=F32)
            + jnp.dot(b_ref[...], theirs, preferred_element_type=F32)
        )
        for ref, others in ((send_ref, (3, 1)), (keep_ref, (2, 0))):
            for to, other in enumerate(others):
                start = pl.multiple_of((quarter ^ other) * share, share)
                ref[to * share : (to + 1) * share, :] = sum_ref[pl.ds(start, share), :].astype(BF16)

    return call(
        kernel,
        [like(rows // 2, width, BF16)] * 2,
        (place, total, across, across_beside, slab),
        scratch=(pltpu.VMEM((rows, width), F32),),
        flops=4 * rows * width * width,
    )


def tiles(late, products, panels, blocks, same, flipped, weight):
    tile, depth = products[0][1].shape
    half, share, n = tile // 2, tile // 4, len(products)
    first = min(steps[0] for _, steps in blocks)
    used = [p for p in range(first, len(panels))]
    parts = [p if isinstance(p, tuple) else (p,) for at in used for p in panels[at]]
    flat = [a for _, a in products] + [a for p in parts for a in p]
    most = max(len(members) for members, _ in blocks)
    widest = max(len(steps) for _, steps in blocks) + 1
    n_out = 2 * bool(same) + 2 * bool(flipped)

    def kernel(late_ref, *refs):
        product_refs = {key: refs[i] for i, (key, _) in enumerate(products)}
        rest, panel_refs = list(refs[n : len(flat)]), []
        for part in parts:
            panel_refs.append(rest[: len(part)])
            rest = rest[len(part) :]
        out_refs, (stack_ref, held_ref) = refs[len(flat) : len(flat) + n_out], refs[-2:]
        for members, steps in blocks:
            rows = len(members) * half
            for i, key in enumerate(members):
                for part in range(2):
                    stack_ref[part, i * half : (i + 1) * half, :] = product_refs[key][
                        part * half : (part + 1) * half, :
                    ]
            for i, step in enumerate((*steps, steps[-1] + 1)):
                halves = [panel_refs[2 * (step - first) + part] for part in range(2)]
                held_ref[:rows, i * tile : (i + 1) * tile] = sum(
                    lax.dot_general(
                        stack_ref[part, :rows, :],
                        half_refs[0][...]
                        if len(half_refs) == 1
                        else jnp.concatenate([ref[...] for ref in half_refs]),
                        TRANSPOSED,
                        preferred_element_type=F32,
                    )
                    for part, half_refs in enumerate(halves)
                )
            for into, (names, kinds) in enumerate(((same, (BF16, F32)), (flipped, (BF16, BF16)))):
                for slot, (key, step) in enumerate(names):
                    if key not in members or not (step in steps or step == WIDE):
                        continue
                    i = members.index(key)
                    column = step - steps[0]
                    if step < WIDE:
                        column = column + late_ref[key]
                    at = pl.ds(pl.multiple_of(column * tile, tile), tile)
                    theirs = held_ref[i * half : i * half + share, at]
                    ours = held_ref[i * half + share : (i + 1) * half, at]
                    pair = (ours, theirs) if into else (theirs, ours)
                    for ref, value, kind in zip(out_refs[2 * into * bool(same) :], pair, kinds):
                        ref[:, slot * tile : (slot + 1) * tile] = value.astype(kind)

    out = []
    if same:
        out += [like(share, len(same) * tile, BF16), like(share, len(same) * tile, F32)]
    if flipped:
        out += [like(share, len(flipped) * tile, BF16)] * 2
    flops = weight * 2 * half * 2 * depth * tile * (len(same) + len(flipped))
    return call(
        kernel,
        out,
        (late, *flat),
        scratch=(
            pltpu.VMEM((2, most * half, depth), BF16),
            pltpu.VMEM((most * half, widest * tile), F32),
        ),
        flops=flops,
    )


def split(sums, groups, tile):
    share = sums[0][0].shape[0]
    flat = [a for pair in sums for a in pair]

    def kernel(_, *refs):
        for ref, group in zip(refs[len(flat) :], groups):
            for to, (which, slot) in enumerate(group):
                left, right = refs[2 * which : 2 * which + 2]
                at = slice(slot * tile, (slot + 1) * tile)
                value = left[:, at].astype(F32) + right[:, at].astype(F32)
                ref[:, to * tile : (to + 1) * tile] = value.astype(ref.dtype)

    return call(
        kernel,
        [
            like(share, len(group) * tile, BF16 if index else F32)
            for index, group in enumerate(groups)
        ],
        (jnp.zeros((1,), jnp.int32), *flat),
    )


def assemble(place, arrays, plan, band, share, tile, base=None):
    count = sum(len(entries) for entries in plan)

    def tiles_of(place_ref, refs):
        low, keep_last = place_ref[0], place_ref[1]
        for ref, entries in zip(refs, plan):
            for slot, entry in enumerate(entries):
                value = ref[:, slot * tile : (slot + 1) * tile].astype(F32)
                if entry is None:
                    yield band - 1, jnp.where(keep_last > 0, value, jnp.zeros_like(value))
                    continue
                flipped, distance, step = entry
                offset = 2 * distance
                if flipped:
                    offset = (offset + 1 - 2 * low) & 7
                yield offset + 8 * step, value

    out = jax.ShapeDtypeStruct((band, share, tile), F32)
    if base is None:

        def first_kernel(place_ref, *refs):
            for offset, value in tiles_of(place_ref, refs[:-1]):
                refs[-1][offset] = value

        return call(first_kernel, out, (place, *arrays))

    def kernel(place_ref, *refs):
        out_ref, stage_ref, sems = refs[-3:]
        copies = []
        for index, (offset, value) in enumerate(tiles_of(place_ref, refs[:-4])):
            stage_ref[index] = value
            copies.append(
                pltpu.make_async_copy(stage_ref.at[index], out_ref.at[offset], sems.at[index])
            )
            copies[-1].start()
        for copy in copies:
            copy.wait()

    anywhere = pl.BlockSpec(memory_space=pl.ANY)
    return pl.pallas_call(
        kernel,
        out_shape=out,
        in_specs=[SMEM] + [VMEM] * len(arrays) + [anywhere],
        out_specs=anywhere,
        input_output_aliases={len(arrays) + 1: 0},
        scratch_shapes=[
            pltpu.VMEM((count, share, tile), F32),
            pltpu.SemaphoreType.DMA((count,)),
        ],
        compiler_params=pltpu.CompilerParams(vmem_limit_bytes=16 * 2**20),
    )(place, *arrays, base)


def per_device(coefficients, jacobi_matrix, jac_limit):
    tile, width = coefficients.shape
    share = tile // 4
    z, x, l, h, c = (lax.axis_index(name) for name in "zxlhc")
    quarter = 2 * h + c
    hold = lax.optimization_barrier

    columns = quarter * width + lax.broadcasted_iota(jnp.int32, (tile, width), 1)
    masked = jnp.where(columns < jac_limit[:, None], coefficients, jnp.zeros_like(coefficients))

    across = shift(masked, "h", 1)
    panels = [masked, shift(masked, "z", 1)]
    beside = shift(masked, "c", 1)

    def rows_of(index):
        return lax.dynamic_slice_in_dim(jacobi_matrix, index * width, width, 0)

    total = jnp.dot(masked, rows_of(quarter), preferred_element_type=F32)
    total = total + jnp.dot(beside, rows_of(quarter ^ 1), preferred_element_type=F32)
    slab = lax.dynamic_slice_in_dim(jacobi_matrix, (1 - h) * 2 * width, 2 * width, 0)
    total, across, slab, panels[1] = hold((total, across, slab, panels[1]))
    across_beside = shift(across, "c", 1)
    place = jnp.stack([c, quarter]).astype(jnp.int32)
    send, keep = own_product(place, total, across, across_beside, slab)
    product = jnp.concatenate([keep, shift(send, "c", 1)])

    def late(dx, flipped):
        return (2 * ((x + dx) % 4) + (l ^ flipped) > 2 * x + l).astype(jnp.int32)

    distances = (0, 1, -1, 2)
    lates = jnp.stack([late(dx, f) for f in (0, 1) for dx in distances])

    def start(products, panels, blocks, same, flipped, weight):
        flipped = [(4 + d, e) for d, e in flipped]
        return tiles(lates, list(products.items()), panels, blocks, same, flipped, weight)

    def finish(sums, names, targets):
        groups = [
            [(n, s) for n, (_, name) in enumerate(names) for s, (d, _) in enumerate(name) if d == to]
            for to in targets
        ]
        pieces = split(sums, groups, tile)
        arrays, plan = [], []
        for to, piece, group in zip(targets, pieces, groups):
            if to:
                piece = shift(piece, "x", -distances[to])
            arrays.append(piece)
            entries = [(names[n][0], names[n][1][s][1]) for n, s in group]
            plan.append([None if e == WIDE else (f, -distances[to] % 4, e) for f, e in entries])
        return arrays, plan

    panels.append(shift(panels[-1], "z", 1))
    flip = shift(product, "l", 1)
    up, down = shift(product, "x", 1), shift(product, "x", -1)

    flip, up, down, panels[2] = hold((flip, up, down, panels[2]))
    panels.append(shift(panels[-1], "z", 1))
    up_flip, down_flip = shift(up, "l", 1), shift(flip, "x", -1)
    far = shift(up, "x", 1)
    both = [(masked, beside)] + [(p, shift(p, "c", 1)) for p in panels[1:3]]

    up_flip, down_flip, far = hold((up_flip, down_flip, far))
    far_flip = shift(down_flip, "x", -1)
    fourth = shift(panels[3], "z", 1)
    both.append((panels[3], shift(panels[3], "c", 1)))
    same_1 = [(d, e) for d in range(4) for e in range(3)]
    products = {0: product, 1: up, 2: down, 3: far}
    other, own = start(products, both, [((0, 1, 2, 3), (0, 1, 2))], same_1, [], 8)

    flipped_1 = [(d, e) for d in range(3) for e in range(3)]
    flip, _ = hold((flip, other))
    other = shift(other, "h", 1)
    products = {4: flip, 5: up_flip, 6: down_flip}
    by_l, by_both = start(products, both, [((4, 5, 6), (0, 1, 2))], [], flipped_1, 8)
    by_l, by_both = shift(by_l, "l", 1), across_and_flip(by_both)

    both.append((fourth, tuple(shift(rows, "c", 1) for rows in jnp.split(fourth, 2))))
    same_2 = [(0, 3), (1, 3), (2, 3), (3, 3), (0, 4)]
    flipped_2 = [(0, 3), (1, 3), (2, 3), (3, 3), (3, 0), (3, 1), (3, 2)]
    products = {0: product, 1: up, 2: down, 3: far, **products, 7: far_flip}
    blocks = [(tuple(range(8)), (3,)), ((7,), (0, 1, 2))]
    other_2, own_2, by_l_2, by_both_2 = start(products, both, blocks, same_2, flipped_2, 0)
    other, by_l, by_both, other_2, by_l_2, by_both_2 = hold(
        (other, by_l, by_both, other_2, by_l_2, by_both_2)
    )
    other_2 = shift(other_2, "h", 1)
    by_l_2, by_both_2 = shift(by_l_2, "l", 1), across_and_flip(by_both_2)
    sums, names = [(own, other), (by_l, by_both)], [(0, same_1), (1, flipped_1)]
    arrays, plan = finish(sums, names, (0, 1, 2))
    other_2, by_l_2, by_both_2, *arrays = hold((other_2, by_l_2, by_both_2, *arrays))
    sums += [(own_2, other_2), (by_l_2, by_both_2)]
    names = [(f, [(d if d == 3 else -1, e) for d, e in name]) for f, name in names]
    names += [(0, same_2), (1, flipped_2)]
    more, more_plan = finish(sums, names, (0, 1, 2, 3))

    where = jnp.stack([l, (z < lax.axis_size("z") // 2)]).astype(jnp.int32)
    band = 8 * WIDE + 1
    out = assemble(where, arrays, plan, band, share, tile)
    out = assemble(where, more, more_plan, band, share, tile, out)
    return jnp.transpose(out, (1, 0, 2))


def solution(mesh):
    fine = Mesh(mesh.devices.reshape(8, 4, 2, 2, 2), ("z", "x", "l", "h", "c"))
    blk, jac = ("z", "x", "l"), ("h", "c")
    in_specs = (P(blk, jac), P(None, jac), P(blk))
    out_specs = P(blk + jac, None, None)
    return jax.shard_map(
        per_device, mesh=fine, in_specs=in_specs, out_specs=out_specs, check_vma=False
    )
```

```python
import jax
import jax.numpy as jnp
from jax import lax
from jax.experimental import pallas as pl
from jax.experimental.pallas import tpu as pltpu
from jax.sharding import Mesh, PartitionSpec as P

WIDE = 4
VMEM = pl.BlockSpec(memory_space=pltpu.VMEM)
SMEM = pl.BlockSpec(memory_space=pltpu.SMEM)
BF16, F32 = jnp.bfloat16, jnp.float32
TRANSPOSED = (((1,), (1,)), ((), ()))


def shift(block, axis, distance):
    n = lax.axis_size(axis)
    return lax.ppermute(block, axis, [((i + distance) % n, i) for i in range(n)])


def across_and_flip(block):
    return lax.ppermute(block, ("l", "h"), [(i, 3 - i) for i in range(4)])


def call(kernel, out_shape, args, scratch=(), flops=0, limit=20):
    moved = sum(a.size * a.dtype.itemsize for a in args)
    return pl.pallas_call(
        kernel,
        out_shape=out_shape,
        in_specs=[SMEM] + [VMEM] * (len(args) - 1),
        out_specs=jax.tree.map(lambda _: VMEM, out_shape),
        scratch_shapes=list(scratch),
        compiler_params=pltpu.CompilerParams(vmem_limit_bytes=limit * 2**20),
        cost_estimate=pl.CostEstimate(flops=flops, bytes_accessed=moved, transcendentals=0),
    )(*args)


def like(rows, columns, dtype):
    return jax.ShapeDtypeStruct((rows, columns), dtype)


def own_product(place, total, across, across_beside, slab):
    rows, width = total.shape
    share = rows // 4

    def kernel(place_ref, total_ref, a_ref, b_ref, slab_ref, send_ref, keep_ref, sum_ref):
        core, quarter = place_ref[0], place_ref[1]
        mine = slab_ref[pl.ds(pl.multiple_of(core * width, width), width), :]
        theirs = slab_ref[pl.ds(pl.multiple_of((1 - core) * width, width), width), :]
        sum_ref[...] = (
            total_ref[...]
            + jnp.dot(a_ref[...], mine, preferred_element_type=F32)
            + jnp.dot(b_ref[...], theirs, preferred_element_type=F32)
        )
        for ref, others in ((send_ref, (3, 1)), (keep_ref, (2, 0))):
            for to, other in enumerate(others):
                start = pl.multiple_of((quarter ^ other) * share, share)
                ref[to * share : (to + 1) * share, :] = sum_ref[pl.ds(start, share), :].astype(BF16)

    return call(
        kernel,
        [like(rows // 2, width, BF16)] * 2,
        (place, total, across, across_beside, slab),
        scratch=(pltpu.VMEM((rows, width), F32),),
        flops=4 * rows * width * width,
    )


def tiles(late, products, panels, blocks, same, flipped, weight):
    tile, depth = products[0][1].shape
    half, share, n = tile // 2, tile // 4, len(products)
    first = min(steps[0] for _, steps in blocks)
    used = [p for p in range(first, len(panels))]
    parts = [p if isinstance(p, tuple) else (p,) for at in used for p in panels[at]]
    flat = [a for _, a in products] + [a for p in parts for a in p]
    most = max(len(members) for members, _ in blocks)
    widest = max(len(steps) for _, steps in blocks) + 1
    n_out = 2 * bool(same) + 2 * bool(flipped)

    def kernel(late_ref, *refs):
        product_refs = {key: refs[i] for i, (key, _) in enumerate(products)}
        rest, panel_refs = list(refs[n : len(flat)]), []
        for part in parts:
            panel_refs.append(rest[: len(part)])
            rest = rest[len(part) :]
        out_refs, (stack_ref, held_ref) = refs[len(flat) : len(flat) + n_out], refs[-2:]
        for members, steps in blocks:
            rows = len(members) * half
            for i, key in enumerate(members):
                for part in range(2):
                    stack_ref[part, i * half : (i + 1) * half, :] = product_refs[key][
                        part * half : (part + 1) * half, :
                    ]
            for i, step in enumerate((*steps, steps[-1] + 1)):
                halves = [panel_refs[2 * (step - first) + part] for part in range(2)]
                held_ref[:rows, i * tile : (i + 1) * tile] = sum(
                    lax.dot_general(
                        stack_ref[part, :rows, :],
                        half_refs[0][...]
                        if len(half_refs) == 1
                        else jnp.concatenate([ref[...] for ref in half_refs]),
                        TRANSPOSED,
                        preferred_element_type=F32,
                    )
                    for part, half_refs in enumerate(halves)
                )
            for into, (names, kinds) in enumerate(((same, (BF16, F32)), (flipped, (BF16, BF16)))):
                for slot, (key, step) in enumerate(names):
                    if key not in members or not (step in steps or step == WIDE):
                        continue
                    i = members.index(key)
                    column = step - steps[0]
                    if step < WIDE:
                        column = column + late_ref[key]
                    at = pl.ds(pl.multiple_of(column * tile, tile), tile)
                    theirs = held_ref[i * half : i * half + share, at]
                    ours = held_ref[i * half + share : (i + 1) * half, at]
                    pair = (ours, theirs) if into else (theirs, ours)
                    for ref, value, kind in zip(out_refs[2 * into * bool(same) :], pair, kinds):
                        ref[:, slot * tile : (slot + 1) * tile] = value.astype(kind)

    out = []
    if same:
        out += [like(share, len(same) * tile, BF16), like(share, len(same) * tile, F32)]
    if flipped:
        out += [like(share, len(flipped) * tile, BF16)] * 2
    flops = weight * 2 * half * 2 * depth * tile * (len(same) + len(flipped))
    return call(
        kernel,
        out,
        (late, *flat),
        scratch=(
            pltpu.VMEM((2, most * half, depth), BF16),
            pltpu.VMEM((most * half, widest * tile), F32),
        ),
        flops=flops,
    )


def split(sums, groups, tile):
    share = sums[0][0].shape[0]
    flat = [a for pair in sums for a in pair]

    def kernel(_, *refs):
        for ref, group in zip(refs[len(flat) :], groups):
            for to, (which, slot) in enumerate(group):
                left, right = refs[2 * which : 2 * which + 2]
                at = slice(slot * tile, (slot + 1) * tile)
                value = left[:, at].astype(F32) + right[:, at].astype(F32)
                ref[:, to * tile : (to + 1) * tile] = value.astype(ref.dtype)

    return call(
        kernel,
        [
            like(share, len(group) * tile, BF16 if index else F32)
            for index, group in enumerate(groups)
        ],
        (jnp.zeros((1,), jnp.int32), *flat),
    )


def assemble(place, arrays, plan, band, share, tile, base=None):
    count = sum(len(entries) for entries in plan)

    def tiles_of(place_ref, refs):
        low, keep_last = place_ref[0], place_ref[1]
        for ref, entries in zip(refs, plan):
            for slot, entry in enumerate(entries):
                value = ref[:, slot * tile : (slot + 1) * tile].astype(F32)
                if entry is None:
                    yield band - 1, jnp.where(keep_last > 0, value, jnp.zeros_like(value))
                    continue
                flipped, distance, step = entry
                offset = 2 * distance
                if flipped:
                    offset = (offset + 1 - 2 * low) & 7
                yield offset + 8 * step, value

    out = jax.ShapeDtypeStruct((band, share, tile), F32)
    if base is None:

        def first_kernel(place_ref, *refs):
            for offset, value in tiles_of(place_ref, refs[:-1]):
                refs[-1][offset] = value

        return call(first_kernel, out, (place, *arrays))

    def kernel(place_ref, *refs):
        out_ref, stage_ref, sems = refs[-3:]
        copies = []
        for index, (offset, value) in enumerate(tiles_of(place_ref, refs[:-4])):
            stage_ref[index] = value
            copies.append(
                pltpu.make_async_copy(stage_ref.at[index], out_ref.at[offset], sems.at[index])
            )
            copies[-1].start()
        for copy in copies:
            copy.wait()

    anywhere = pl.BlockSpec(memory_space=pl.ANY)
    return pl.pallas_call(
        kernel,
        out_shape=out,
        in_specs=[SMEM] + [VMEM] * len(arrays) + [anywhere],
        out_specs=anywhere,
        input_output_aliases={len(arrays) + 1: 0},
        scratch_shapes=[
            pltpu.VMEM((count, share, tile), F32),
            pltpu.SemaphoreType.DMA((count,)),
        ],
        compiler_params=pltpu.CompilerParams(vmem_limit_bytes=16 * 2**20),
    )(place, *arrays, base)


def per_device(coefficients, jacobi_matrix, jac_limit):
    tile, width = coefficients.shape
    share = tile // 4
    z, x, l, h, c = (lax.axis_index(name) for name in "zxlhc")
    quarter = 2 * h + c
    hold = lax.optimization_barrier

    columns = quarter * width + lax.broadcasted_iota(jnp.int32, (tile, width), 1)
    masked = jnp.where(columns < jac_limit[:, None], coefficients, jnp.zeros_like(coefficients))

    across = shift(masked, "h", 1)
    panels = [masked, shift(masked, "z", 1)]
    beside = shift(masked, "c", 1)

    def rows_of(index):
        return lax.dynamic_slice_in_dim(jacobi_matrix, index * width, width, 0)

    total = jnp.dot(masked, rows_of(quarter), preferred_element_type=F32)
    total = total + jnp.dot(beside, rows_of(quarter ^ 1), preferred_element_type=F32)
    slab = lax.dynamic_slice_in_dim(jacobi_matrix, (1 - h) * 2 * width, 2 * width, 0)
    total, across, slab, panels[1] = hold((total, across, slab, panels[1]))
    across_beside = shift(across, "c", 1)
    place = jnp.stack([c, quarter]).astype(jnp.int32)
    send, keep = own_product(place, total, across, across_beside, slab)
    product = jnp.concatenate([keep, shift(send, "c", 1)])

    def late(dx, flipped):
        return (2 * ((x + dx) % 4) + (l ^ flipped) > 2 * x + l).astype(jnp.int32)

    distances = (0, 1, -1, 2)
    lates = jnp.stack([late(dx, f) for f in (0, 1) for dx in distances])

    def start(products, panels, blocks, same, flipped, weight):
        flipped = [(4 + d, e) for d, e in flipped]
        return tiles(lates, list(products.items()), panels, blocks, same, flipped, weight)

    def finish(sums, names, targets):
        groups = [
            [(n, s) for n, (_, name) in enumerate(names) for s, (d, _) in enumerate(name) if d == to]
            for to in targets
        ]
        pieces = split(sums, groups, tile)
        arrays, plan = [], []
        for to, piece, group in zip(targets, pieces, groups):
            if to:
                piece = shift(piece, "x", -distances[to])
            arrays.append(piece)
            entries = [(names[n][0], names[n][1][s][1]) for n, s in group]
            plan.append([None if e == WIDE else (f, -distances[to] % 4, e) for f, e in entries])
        return arrays, plan

    panels.append(shift(panels[-1], "z", 1))
    flip = shift(product, "l", 1)
    up, down = shift(product, "x", 1), shift(product, "x", -1)

    first = shift(panels[1], "c", 1)
    flip, up, down, panels[2], first = hold((flip, up, down, panels[2], first))
    panels.append(shift(panels[-1], "z", 1))
    up_flip, down_flip = shift(up, "l", 1), shift(flip, "x", -1)
    far = shift(up, "x", 1)
    both = [(masked, beside), (panels[1], first), (panels[2], shift(panels[2], "c", 1))]

    up_flip, far = hold((up_flip, far))
    far_flip = shift(down_flip, "x", -1)
    fourth = shift(panels[3], "z", 1)
    both.append((panels[3], shift(panels[3], "c", 1)))
    same_1 = [(d, e) for d in range(4) for e in range(3)]
    products = {0: product, 1: up, 2: down, 3: far}
    other, own = start(products, both, [((0, 1, 2, 3), (0, 1, 2))], same_1, [], 8)

    flipped_1 = [(d, e) for d in range(3) for e in range(3)]
    flip, _ = hold((flip, other))
    other = shift(other, "h", 1)
    products = {4: flip, 5: up_flip, 6: down_flip}
    by_l, by_both = start(products, both, [((4, 5, 6), (0, 1, 2))], [], flipped_1, 8)
    by_l, by_both = shift(by_l, "l", 1), across_and_flip(by_both)

    both.append((fourth, tuple(shift(rows, "c", 1) for rows in jnp.split(fourth, 2))))
    same_2 = [(0, 3), (1, 3), (2, 3), (3, 3), (0, 4)]
    flipped_2 = [(0, 3), (1, 3), (2, 3), (3, 3), (3, 0), (3, 1), (3, 2)]
    products = {0: product, 1: up, 2: down, 3: far, **products, 7: far_flip}
    blocks = [(tuple(range(8)), (3,)), ((7,), (0, 1, 2))]
    other_2, own_2, by_l_2, by_both_2 = start(products, both, blocks, same_2, flipped_2, 0)
    other, by_l, by_both, other_2, by_l_2, by_both_2 = hold(
        (other, by_l, by_both, other_2, by_l_2, by_both_2)
    )
    other_2 = shift(other_2, "h", 1)
    by_l_2, by_both_2 = shift(by_l_2, "l", 1), across_and_flip(by_both_2)
    sums, names = [(own, other), (by_l, by_both)], [(0, same_1), (1, flipped_1)]
    arrays, plan = finish(sums, names, (0, 1, 2))
    other_2, by_l_2, by_both_2, *arrays = hold((other_2, by_l_2, by_both_2, *arrays))
    sums += [(own_2, other_2), (by_l_2, by_both_2)]
    names = [(f, [(d if d == 3 else -1, e) for d, e in name]) for f, name in names]
    names += [(0, same_2), (1, flipped_2)]
    more, more_plan = finish(sums, names, (0, 1, 2, 3))

    where = jnp.stack([l, (z < lax.axis_size("z") // 2)]).astype(jnp.int32)
    band = 8 * WIDE + 1
    out = assemble(where, arrays, plan, band, share, tile)
    out = assemble(where, more, more_plan, band, share, tile, out)
    return jnp.transpose(out, (1, 0, 2))


def solution(mesh):
    fine = Mesh(mesh.devices.reshape(8, 4, 2, 2, 2), ("z", "x", "l", "h", "c"))
    blk, jac = ("z", "x", "l"), ("h", "c")
    in_specs = (P(blk, jac), P(None, jac), P(blk))
    out_specs = P(blk + jac, None, None)
    return jax.shard_map(
        per_device, mesh=fine, in_specs=in_specs, out_specs=out_specs, check_vma=False
    )
```

```python
import jax
import jax.numpy as jnp
from jax import lax
from jax.experimental import pallas as pl
from jax.experimental.pallas import tpu as pltpu
from jax.sharding import Mesh, PartitionSpec as P

WIDE = 4
VMEM = pl.BlockSpec(memory_space=pltpu.VMEM)
SMEM = pl.BlockSpec(memory_space=pltpu.SMEM)
BF16, F32 = jnp.bfloat16, jnp.float32
TRANSPOSED = (((1,), (1,)), ((), ()))


def shift(block, axis, distance):
    n = lax.axis_size(axis)
    return lax.ppermute(block, axis, [((i + distance) % n, i) for i in range(n)])


def across_and_flip(block):
    return lax.ppermute(block, ("l", "h"), [(i, 3 - i) for i in range(4)])


def call(kernel, out_shape, args, scratch=(), flops=0, limit=20):
    moved = sum(a.size * a.dtype.itemsize for a in args)
    return pl.pallas_call(
        kernel,
        out_shape=out_shape,
        in_specs=[SMEM] + [VMEM] * (len(args) - 1),
        out_specs=jax.tree.map(lambda _: VMEM, out_shape),
        scratch_shapes=list(scratch),
        compiler_params=pltpu.CompilerParams(vmem_limit_bytes=limit * 2**20),
        cost_estimate=pl.CostEstimate(flops=flops, bytes_accessed=moved, transcendentals=0),
    )(*args)


def like(rows, columns, dtype):
    return jax.ShapeDtypeStruct((rows, columns), dtype)


def own_product(place, total, across, across_beside, slab):
    rows, width = total.shape
    share = rows // 4

    def kernel(place_ref, total_ref, a_ref, b_ref, slab_ref, send_ref, keep_ref, sum_ref):
        core, quarter = place_ref[0], place_ref[1]
        mine = slab_ref[pl.ds(pl.multiple_of(core * width, width), width), :]
        theirs = slab_ref[pl.ds(pl.multiple_of((1 - core) * width, width), width), :]
        sum_ref[...] = (
            total_ref[...]
            + jnp.dot(a_ref[...], mine, preferred_element_type=F32)
            + jnp.dot(b_ref[...], theirs, preferred_element_type=F32)
        )
        for ref, others in ((send_ref, (3, 1)), (keep_ref, (2, 0))):
            for to, other in enumerate(others):
                start = pl.multiple_of((quarter ^ other) * share, share)
                ref[to * share : (to + 1) * share, :] = sum_ref[pl.ds(start, share), :].astype(BF16)

    return call(
        kernel,
        [like(rows // 2, width, BF16)] * 2,
        (place, total, across, across_beside, slab),
        scratch=(pltpu.VMEM((rows, width), F32),),
        flops=4 * rows * width * width,
    )


def tiles(late, products, panels, blocks, same, flipped, weight):
    tile, depth = products[0][1].shape
    half, share, n = tile // 2, tile // 4, len(products)
    first = min(steps[0] for _, steps in blocks)
    used = [p for p in range(first, len(panels))]
    parts = [p if isinstance(p, tuple) else (p,) for at in used for p in panels[at]]
    flat = [a for _, a in products] + [a for p in parts for a in p]
    most = max(len(members) for members, _ in blocks)
    widest = max(len(steps) for _, steps in blocks) + 1
    n_out = 2 * bool(same) + 2 * bool(flipped)

    def kernel(late_ref, *refs):
        product_refs = {key: refs[i] for i, (key, _) in enumerate(products)}
        rest, panel_refs = list(refs[n : len(flat)]), []
        for part in parts:
            panel_refs.append(rest[: len(part)])
            rest = rest[len(part) :]
        out_refs, (stack_ref, held_ref) = refs[len(flat) : len(flat) + n_out], refs[-2:]
        for members, steps in blocks:
            rows = len(members) * half
            for i, key in enumerate(members):
                for part in range(2):
                    stack_ref[part, i * half : (i + 1) * half, :] = product_refs[key][
                        part * half : (part + 1) * half, :
                    ]
            for i, step in enumerate((*steps, steps[-1] + 1)):
                halves = [panel_refs[2 * (step - first) + part] for part in range(2)]
                held_ref[:rows, i * tile : (i + 1) * tile] = sum(
                    lax.dot_general(
                        stack_ref[part, :rows, :],
                        half_refs[0][...]
                        if len(half_refs) == 1
                        else jnp.concatenate([ref[...] for ref in half_refs]),
                        TRANSPOSED,
                        preferred_element_type=F32,
                    )
                    for part, half_refs in enumerate(halves)
                )
            for into, (names, kinds) in enumerate(((same, (BF16, F32)), (flipped, (BF16, BF16)))):
                for slot, (key, step) in enumerate(names):
                    if key not in members or not (step in steps or step == WIDE):
                        continue
                    i = members.index(key)
                    column = step - steps[0]
                    if step < WIDE:
                        column = column + late_ref[key]
                    at = pl.ds(pl.multiple_of(column * tile, tile), tile)
                    theirs = held_ref[i * half : i * half + share, at]
                    ours = held_ref[i * half + share : (i + 1) * half, at]
                    pair = (ours, theirs) if into else (theirs, ours)
                    for ref, value, kind in zip(out_refs[2 * into * bool(same) :], pair, kinds):
                        ref[:, slot * tile : (slot + 1) * tile] = value.astype(kind)

    out = []
    if same:
        out += [like(share, len(same) * tile, BF16), like(share, len(same) * tile, F32)]
    if flipped:
        out += [like(share, len(flipped) * tile, BF16)] * 2
    flops = weight * 2 * half * 2 * depth * tile * (len(same) + len(flipped))
    return call(
        kernel,
        out,
        (late, *flat),
        scratch=(
            pltpu.VMEM((2, most * half, depth), BF16),
            pltpu.VMEM((most * half, widest * tile), F32),
        ),
        flops=flops,
    )


def split(sums, groups, tile):
    share = sums[0][0].shape[0]
    flat = [a for pair in sums for a in pair]

    def kernel(_, *refs):
        for ref, group in zip(refs[len(flat) :], groups):
            for to, (which, slot) in enumerate(group):
                left, right = refs[2 * which : 2 * which + 2]
                at = slice(slot * tile, (slot + 1) * tile)
                value = left[:, at].astype(F32) + right[:, at].astype(F32)
                ref[:, to * tile : (to + 1) * tile] = value.astype(ref.dtype)

    return call(
        kernel,
        [
            like(share, len(group) * tile, BF16 if index else F32)
            for index, group in enumerate(groups)
        ],
        (jnp.zeros((1,), jnp.int32), *flat),
    )


def assemble(place, arrays, plan, band, share, tile, base=None):
    count = sum(len(entries) for entries in plan)

    def tiles_of(place_ref, refs):
        low, keep_last = place_ref[0], place_ref[1]
        for ref, entries in zip(refs, plan):
            for slot, entry in enumerate(entries):
                value = ref[:, slot * tile : (slot + 1) * tile].astype(F32)
                if entry is None:
                    yield band - 1, jnp.where(keep_last > 0, value, jnp.zeros_like(value))
                    continue
                flipped, distance, step = entry
                offset = 2 * distance
                if flipped:
                    offset = (offset + 1 - 2 * low) & 7
                yield offset + 8 * step, value

    out = jax.ShapeDtypeStruct((band, share, tile), F32)
    if base is None:

        def first_kernel(place_ref, *refs):
            for offset, value in tiles_of(place_ref, refs[:-1]):
                refs[-1][offset] = value

        return call(first_kernel, out, (place, *arrays))

    def kernel(place_ref, *refs):
        out_ref, stage_ref, sems = refs[-3:]
        copies = []
        for index, (offset, value) in enumerate(tiles_of(place_ref, refs[:-4])):
            stage_ref[index] = value
            copies.append(
                pltpu.make_async_copy(stage_ref.at[index], out_ref.at[offset], sems.at[index])
            )
            copies[-1].start()
        for copy in copies:
            copy.wait()

    anywhere = pl.BlockSpec(memory_space=pl.ANY)
    return pl.pallas_call(
        kernel,
        out_shape=out,
        in_specs=[SMEM] + [VMEM] * len(arrays) + [anywhere],
        out_specs=anywhere,
        input_output_aliases={len(arrays) + 1: 0},
        scratch_shapes=[
            pltpu.VMEM((count, share, tile), F32),
            pltpu.SemaphoreType.DMA((count,)),
        ],
        compiler_params=pltpu.CompilerParams(vmem_limit_bytes=16 * 2**20),
    )(place, *arrays, base)


def per_device(coefficients, jacobi_matrix, jac_limit):
    tile, width = coefficients.shape
    share = tile // 4
    z, x, l, h, c = (lax.axis_index(name) for name in "zxlhc")
    quarter = 2 * h + c
    hold = lax.optimization_barrier

    columns = quarter * width + lax.broadcasted_iota(jnp.int32, (tile, width), 1)
    masked = jnp.where(columns < jac_limit[:, None], coefficients, jnp.zeros_like(coefficients))

    across = shift(masked, "h", 1)
    panels = [masked, shift(masked, "z", 1)]
    beside = shift(masked, "c", 1)

    def rows_of(index):
        return lax.dynamic_slice_in_dim(jacobi_matrix, index * width, width, 0)

    total = jnp.dot(masked, rows_of(quarter), preferred_element_type=F32)
    total = total + jnp.dot(beside, rows_of(quarter ^ 1), preferred_element_type=F32)
    slab = lax.dynamic_slice_in_dim(jacobi_matrix, (1 - h) * 2 * width, 2 * width, 0)
    total, across, slab, panels[1] = hold((total, across, slab, panels[1]))
    across_beside = shift(across, "c", 1)
    place = jnp.stack([c, quarter]).astype(jnp.int32)
    send, keep = own_product(place, total, across, across_beside, slab)
    product = jnp.concatenate([keep, shift(send, "c", 1)])

    def late(dx, flipped):
        return (2 * ((x + dx) % 4) + (l ^ flipped) > 2 * x + l).astype(jnp.int32)

    distances = (0, 1, -1, 2)
    lates = jnp.stack([late(dx, f) for f in (0, 1) for dx in distances])

    def start(products, panels, blocks, same, flipped, weight):
        flipped = [(4 + d, e) for d, e in flipped]
        return tiles(lates, list(products.items()), panels, blocks, same, flipped, weight)

    def finish(sums, names, targets):
        groups = [
            [(n, s) for n, (_, name) in enumerate(names) for s, (d, _) in enumerate(name) if d == to]
            for to in targets
        ]
        pieces = split(sums, groups, tile)
        arrays, plan = [], []
        for to, piece, group in zip(targets, pieces, groups):
            if to:
                piece = shift(piece, "x", -distances[to])
            arrays.append(piece)
            entries = [(names[n][0], names[n][1][s][1]) for n, s in group]
            plan.append([None if e == WIDE else (f, -distances[to] % 4, e) for f, e in entries])
        return arrays, plan

    panels.append(shift(panels[-1], "z", 1))
    flip = shift(product, "l", 1)
    up, down = shift(product, "x", 1), shift(product, "x", -1)

    first = shift(panels[1], "c", 1)
    flip, up, down, panels[2], first = hold((flip, up, down, panels[2], first))
    panels.append(shift(panels[-1], "z", 1))
    up_flip, down_flip = shift(up, "l", 1), shift(flip, "x", -1)
    far = shift(up, "x", 1)
    both = [(masked, beside), (panels[1], first), (panels[2], shift(panels[2], "c", 1))]

    up_flip, far = hold((up_flip, far))
    far_flip = shift(down_flip, "x", -1)
    fourth = shift(panels[3], "z", 1)
    both.append((panels[3], shift(panels[3], "c", 1)))
    same_1 = [(d, e) for d in range(4) for e in range(3)]
    products = {0: product, 1: up, 2: down, 3: far}
    other, own = start(products, both, [((0, 1, 2, 3), (0, 1, 2))], same_1, [], 8)

    flipped_1 = [(d, e) for d in range(3) for e in range(3)]
    flip, _ = hold((flip, other))
    other = shift(other, "h", 1)
    products = {4: flip, 5: up_flip, 6: down_flip}
    by_l, by_both = start(products, both, [((4, 5, 6), (0, 1, 2))], [], flipped_1, 8)
    by_l, by_both = shift(by_l, "l", 1), across_and_flip(by_both)

    both.append((fourth, tuple(shift(rows, "c", 1) for rows in jnp.split(fourth, 2))))
    same_2 = [(0, 3), (1, 3), (2, 3), (3, 3), (0, 4)]
    flipped_2 = [(0, 3), (1, 3), (2, 3), (3, 3), (3, 0), (3, 1), (3, 2)]
    products = {0: product, 1: up, 2: down, 3: far, **products, 7: far_flip}
    blocks = [(tuple(range(8)), (3,)), ((7,), (0, 1, 2))]
    other_2, own_2, by_l_2, by_both_2 = start(products, both, blocks, same_2, flipped_2, 0)
    other, by_l, by_both, other_2, by_l_2, by_both_2 = hold(
        (other, by_l, by_both, other_2, by_l_2, by_both_2)
    )
    other_2 = shift(other_2, "h", 1)
    by_l_2, by_both_2 = shift(by_l_2, "l", 1), across_and_flip(by_both_2)
    sums, names = [(own, other), (by_l, by_both)], [(0, same_1), (1, flipped_1)]
    arrays, plan = finish(sums, names, (0, 1, 2))
    other_2, by_l_2, by_both_2, *arrays = hold((other_2, by_l_2, by_both_2, *arrays))
    sums += [(own_2, other_2), (by_l_2, by_both_2)]
    names = [(f, [(d if d == 3 else -1, e) for d, e in name]) for f, name in names]
    names += [(0, same_2), (1, flipped_2)]
    more, more_plan = finish(sums, names, (0, 1, 2, 3))

    where = jnp.stack([l, (z < lax.axis_size("z") // 2)]).astype(jnp.int32)
    band = 8 * WIDE + 1
    out = assemble(where, [*arrays, more[0]], [*plan, more_plan[0]], band, share, tile)
    out = assemble(where, more[1:], more_plan[1:], band, share, tile, out)
    return jnp.transpose(out, (1, 0, 2))


def solution(mesh):
    fine = Mesh(mesh.devices.reshape(8, 4, 2, 2, 2), ("z", "x", "l", "h", "c"))
    blk, jac = ("z", "x", "l"), ("h", "c")
    in_specs = (P(blk, jac), P(None, jac), P(blk))
    out_specs = P(blk + jac, None, None)
    return jax.shard_map(
        per_device, mesh=fine, in_specs=in_specs, out_specs=out_specs, check_vma=False
    )
```

```python
import jax
import jax.numpy as jnp
from jax import lax
from jax.experimental import pallas as pl
from jax.experimental.pallas import tpu as pltpu
from jax.sharding import Mesh, PartitionSpec as P

WIDE = 4
VMEM = pl.BlockSpec(memory_space=pltpu.VMEM)
SMEM = pl.BlockSpec(memory_space=pltpu.SMEM)
BF16, F32 = jnp.bfloat16, jnp.float32
TRANSPOSED = (((1,), (1,)), ((), ()))


def shift(block, axis, distance):
    n = lax.axis_size(axis)
    return lax.ppermute(block, axis, [((i + distance) % n, i) for i in range(n)])


def across_and_flip(block):
    return lax.ppermute(block, ("l", "h"), [(i, 3 - i) for i in range(4)])


def call(kernel, out_shape, args, scratch=(), flops=0, limit=20):
    moved = sum(a.size * a.dtype.itemsize for a in args)
    return pl.pallas_call(
        kernel,
        out_shape=out_shape,
        in_specs=[SMEM] + [VMEM] * (len(args) - 1),
        out_specs=jax.tree.map(lambda _: VMEM, out_shape),
        scratch_shapes=list(scratch),
        compiler_params=pltpu.CompilerParams(vmem_limit_bytes=limit * 2**20),
        cost_estimate=pl.CostEstimate(flops=flops, bytes_accessed=moved, transcendentals=0),
    )(*args)


def like(rows, columns, dtype):
    return jax.ShapeDtypeStruct((rows, columns), dtype)


def own_product(place, total, across, across_beside, slab):
    rows, width = total.shape
    share = rows // 4

    def kernel(place_ref, total_ref, a_ref, b_ref, slab_ref, send_ref, keep_ref, sum_ref):
        core, quarter = place_ref[0], place_ref[1]
        mine = slab_ref[pl.ds(pl.multiple_of(core * width, width), width), :]
        theirs = slab_ref[pl.ds(pl.multiple_of((1 - core) * width, width), width), :]
        sum_ref[...] = (
            total_ref[...]
            + jnp.dot(a_ref[...], mine, preferred_element_type=F32)
            + jnp.dot(b_ref[...], theirs, preferred_element_type=F32)
        )
        for ref, others in ((send_ref, (3, 1)), (keep_ref, (2, 0))):
            for to, other in enumerate(others):
                start = pl.multiple_of((quarter ^ other) * share, share)
                ref[to * share : (to + 1) * share, :] = sum_ref[pl.ds(start, share), :].astype(BF16)

    return call(
        kernel,
        [like(rows // 2, width, BF16)] * 2,
        (place, total, across, across_beside, slab),
        scratch=(pltpu.VMEM((rows, width), F32),),
        flops=4 * rows * width * width,
    )


def tiles(late, products, panels, blocks, same, flipped, weight):
    tile, depth = products[0][1].shape
    half, share, n = tile // 2, tile // 4, len(products)
    first = min(steps[0] for _, steps in blocks)
    used = [p for p in range(first, len(panels))]
    parts = [p if isinstance(p, tuple) else (p,) for at in used for p in panels[at]]
    flat = [a for _, a in products] + [a for p in parts for a in p]
    most = max(len(members) for members, _ in blocks)
    widest = max(len(steps) for _, steps in blocks) + 1
    n_out = 2 * bool(same) + 2 * bool(flipped)

    def kernel(late_ref, *refs):
        product_refs = {key: refs[i] for i, (key, _) in enumerate(products)}
        rest, panel_refs = list(refs[n : len(flat)]), []
        for part in parts:
            panel_refs.append(rest[: len(part)])
            rest = rest[len(part) :]
        out_refs, (stack_ref, held_ref) = refs[len(flat) : len(flat) + n_out], refs[-2:]
        for members, steps in blocks:
            rows = len(members) * half
            for i, key in enumerate(members):
                for part in range(2):
                    stack_ref[part, i * half : (i + 1) * half, :] = product_refs[key][
                        part * half : (part + 1) * half, :
                    ]
            for i, step in enumerate((*steps, steps[-1] + 1)):
                halves = [panel_refs[2 * (step - first) + part] for part in range(2)]
                low = half if members[0] == 0 and step not in steps and (0, WIDE) not in same else 0
                held_ref[low:rows, i * tile : (i + 1) * tile] = sum(
                    lax.dot_general(
                        stack_ref[part, low:rows, :],
                        half_refs[0][...]
                        if len(half_refs) == 1
                        else jnp.concatenate([ref[...] for ref in half_refs]),
                        TRANSPOSED,
                        preferred_element_type=F32,
                    )
                    for part, half_refs in enumerate(halves)
                )
            for into, (names, kinds) in enumerate(((same, (BF16, F32)), (flipped, (BF16, BF16)))):
                for slot, (key, step) in enumerate(names):
                    if key not in members or not (step in steps or step == WIDE):
                        continue
                    i = members.index(key)
                    column = step - steps[0]
                    if step < WIDE:
                        column = column + late_ref[key]
                    at = pl.ds(pl.multiple_of(column * tile, tile), tile)
                    theirs = held_ref[i * half : i * half + share, at]
                    ours = held_ref[i * half + share : (i + 1) * half, at]
                    pair = (ours, theirs) if into else (theirs, ours)
                    for ref, value, kind in zip(out_refs[2 * into * bool(same) :], pair, kinds):
                        ref[:, slot * tile : (slot + 1) * tile] = value.astype(kind)

    out = []
    if same:
        out += [like(share, len(same) * tile, BF16), like(share, len(same) * tile, F32)]
    if flipped:
        out += [like(share, len(flipped) * tile, BF16)] * 2
    flops = weight * 2 * half * 2 * depth * tile * (len(same) + len(flipped))
    return call(
        kernel,
        out,
        (late, *flat),
        scratch=(
            pltpu.VMEM((2, most * half, depth), BF16),
            pltpu.VMEM((most * half, widest * tile), F32),
        ),
        flops=flops,
    )


def split(sums, groups, tile):
    share = sums[0][0].shape[0]
    flat = [a for pair in sums for a in pair]

    def kernel(_, *refs):
        for ref, group in zip(refs[len(flat) :], groups):
            for to, (which, slot) in enumerate(group):
                left, right = refs[2 * which : 2 * which + 2]
                at = slice(slot * tile, (slot + 1) * tile)
                value = left[:, at].astype(F32) + right[:, at].astype(F32)
                ref[:, to * tile : (to + 1) * tile] = value.astype(ref.dtype)

    return call(
        kernel,
        [
            like(share, len(group) * tile, BF16 if index else F32)
            for index, group in enumerate(groups)
        ],
        (jnp.zeros((1,), jnp.int32), *flat),
    )


def assemble(place, arrays, plan, band, share, tile, base=None):
    count = sum(len(entries) for entries in plan)

    def tiles_of(place_ref, refs):
        low, keep_last = place_ref[0], place_ref[1]
        for ref, entries in zip(refs, plan):
            for slot, entry in enumerate(entries):
                value = ref[:, slot * tile : (slot + 1) * tile].astype(F32)
                if entry is None:
                    yield band - 1, jnp.where(keep_last > 0, value, jnp.zeros_like(value))
                    continue
                flipped, distance, step = entry
                offset = 2 * distance
                if flipped:
                    offset = (offset + 1 - 2 * low) & 7
                yield offset + 8 * step, value

    out = jax.ShapeDtypeStruct((band, share, tile), F32)
    if base is None:

        def first_kernel(place_ref, *refs):
            for offset, value in tiles_of(place_ref, refs[:-1]):
                refs[-1][offset] = value

        return call(first_kernel, out, (place, *arrays))

    def kernel(place_ref, *refs):
        out_ref, stage_ref, sems = refs[-3:]
        copies = []
        for index, (offset, value) in enumerate(tiles_of(place_ref, refs[:-4])):
            stage_ref[index] = value
            copies.append(
                pltpu.make_async_copy(stage_ref.at[index], out_ref.at[offset], sems.at[index])
            )
            copies[-1].start()
        for copy in copies:
            copy.wait()

    anywhere = pl.BlockSpec(memory_space=pl.ANY)
    return pl.pallas_call(
        kernel,
        out_shape=out,
        in_specs=[SMEM] + [VMEM] * len(arrays) + [anywhere],
        out_specs=anywhere,
        input_output_aliases={len(arrays) + 1: 0},
        scratch_shapes=[
            pltpu.VMEM((count, share, tile), F32),
            pltpu.SemaphoreType.DMA((count,)),
        ],
        compiler_params=pltpu.CompilerParams(vmem_limit_bytes=16 * 2**20),
    )(place, *arrays, base)


def per_device(coefficients, jacobi_matrix, jac_limit):
    tile, width = coefficients.shape
    share = tile // 4
    z, x, l, h, c = (lax.axis_index(name) for name in "zxlhc")
    quarter = 2 * h + c
    hold = lax.optimization_barrier

    columns = quarter * width + lax.broadcasted_iota(jnp.int32, (tile, width), 1)
    masked = jnp.where(columns < jac_limit[:, None], coefficients, jnp.zeros_like(coefficients))

    across = shift(masked, "h", 1)
    panels = [masked, shift(masked, "z", 1)]
    beside = shift(masked, "c", 1)

    def rows_of(index):
        return lax.dynamic_slice_in_dim(jacobi_matrix, index * width, width, 0)

    total = jnp.dot(masked, rows_of(quarter), preferred_element_type=F32)
    total = total + jnp.dot(beside, rows_of(quarter ^ 1), preferred_element_type=F32)
    slab = lax.dynamic_slice_in_dim(jacobi_matrix, (1 - h) * 2 * width, 2 * width, 0)
    total, across, slab, panels[1] = hold((total, across, slab, panels[1]))
    across_beside = shift(across, "c", 1)
    place = jnp.stack([c, quarter]).astype(jnp.int32)
    send, keep = own_product(place, total, across, across_beside, slab)
    product = jnp.concatenate([keep, shift(send, "c", 1)])

    def late(dx, flipped):
        return (2 * ((x + dx) % 4) + (l ^ flipped) > 2 * x + l).astype(jnp.int32)

    distances = (0, 1, -1, 2)
    lates = jnp.stack([late(dx, f) for f in (0, 1) for dx in distances])

    def start(products, panels, blocks, same, flipped, weight):
        flipped = [(4 + d, e) for d, e in flipped]
        return tiles(lates, list(products.items()), panels, blocks, same, flipped, weight)

    def finish(sums, names, targets):
        groups = [
            [(n, s) for n, (_, name) in enumerate(names) for s, (d, _) in enumerate(name) if d == to]
            for to in targets
        ]
        pieces = split(sums, groups, tile)
        arrays, plan = [], []
        for to, piece, group in zip(targets, pieces, groups):
            if to:
                piece = shift(piece, "x", -distances[to])
            arrays.append(piece)
            entries = [(names[n][0], names[n][1][s][1]) for n, s in group]
            plan.append([None if e == WIDE else (f, -distances[to] % 4, e) for f, e in entries])
        return arrays, plan

    panels.append(shift(panels[-1], "z", 1))
    flip = shift(product, "l", 1)
    up, down = shift(product, "x", 1), shift(product, "x", -1)

    first = shift(panels[1], "c", 1)
    flip, up, down, panels[2], first = hold((flip, up, down, panels[2], first))
    panels.append(shift(panels[-1], "z", 1))
    up_flip, down_flip = shift(up, "l", 1), shift(flip, "x", -1)
    far = shift(up, "x", 1)
    both = [(masked, beside), (panels[1], first), (panels[2], shift(panels[2], "c", 1))]

    up_flip, far = hold((up_flip, far))
    far_flip = shift(down_flip, "x", -1)
    fourth = shift(panels[3], "z", 1)
    both.append((panels[3], shift(panels[3], "c", 1)))
    same_1 = [(d, e) for d in range(4) for e in range(3)]
    products = {0: product, 1: up, 2: down, 3: far}
    other, own = start(products, both, [((0, 1, 2, 3), (0, 1, 2))], same_1, [], 8)

    flipped_1 = [(d, e) for d in range(3) for e in range(3)]
    flip, _ = hold((flip, other))
    other = shift(other, "h", 1)
    products = {4: flip, 5: up_flip, 6: down_flip}
    by_l, by_both = start(products, both, [((4, 5, 6), (0, 1, 2))], [], flipped_1, 8)
    by_l, by_both = shift(by_l, "l", 1), across_and_flip(by_both)

    both.append((fourth, tuple(shift(rows, "c", 1) for rows in jnp.split(fourth, 2))))
    same_2 = [(0, 3), (1, 3), (2, 3), (3, 3), (0, 4)]
    flipped_2 = [(0, 3), (1, 3), (2, 3), (3, 3), (3, 0), (3, 1), (3, 2)]
    products = {0: product, 1: up, 2: down, 3: far, **products, 7: far_flip}
    blocks = [(tuple(range(8)), (3,)), ((7,), (0, 1, 2))]
    other_2, own_2, by_l_2, by_both_2 = start(products, both, blocks, same_2, flipped_2, 0)
    other, by_l, by_both, other_2, by_l_2, by_both_2 = hold(
        (other, by_l, by_both, other_2, by_l_2, by_both_2)
    )
    other_2 = shift(other_2, "h", 1)
    by_l_2, by_both_2 = shift(by_l_2, "l", 1), across_and_flip(by_both_2)
    sums, names = [(own, other), (by_l, by_both)], [(0, same_1), (1, flipped_1)]
    arrays, plan = finish(sums, names, (0, 1, 2))
    other_2, by_l_2, by_both_2, *arrays = hold((other_2, by_l_2, by_both_2, *arrays))
    sums += [(own_2, other_2), (by_l_2, by_both_2)]
    names = [(f, [(d if d == 3 else -1, e) for d, e in name]) for f, name in names]
    names += [(0, same_2), (1, flipped_2)]
    more, more_plan = finish(sums, names, (0, 1, 2, 3))

    where = jnp.stack([l, (z < lax.axis_size("z") // 2)]).astype(jnp.int32)
    band = 8 * WIDE + 1
    out = assemble(where, arrays, plan, band, share, tile)
    out = assemble(where, more, more_plan, band, share, tile, out)
    return jnp.transpose(out, (1, 0, 2))


def solution(mesh):
    fine = Mesh(mesh.devices.reshape(8, 4, 2, 2, 2), ("z", "x", "l", "h", "c"))
    blk, jac = ("z", "x", "l"), ("h", "c")
    in_specs = (P(blk, jac), P(None, jac), P(blk))
    out_specs = P(blk + jac, None, None)
    return jax.shard_map(
        per_device, mesh=fine, in_specs=in_specs, out_specs=out_specs, check_vma=False
    )
```
